512 devices in a mesh: atlas: 4 (over y), row: 32 (over z, core), col: 4 (over x).
Axes of the slice: x: 4, y: 4, z: 16, core: 2. Of those that a mesh axis runs over, the one named last changes fastest.
Arguments:
- cells: bfloat16 [4, 64, 16384], P('atlas', None, 'row'), may hold values from -4 to 4
- support: bfloat16 [64, 16384], P(None, 'col'), may hold values from -4 to 4
Outputs:
- cell_dual: float32 [4, 16384], P('atlas', 'row')
- support_dual: float32 [4, 16384], P('atlas', 'col')
- new_support: float32 [64, 16384], P(None, 'col')
The draws below stay inside these ranges and needn't reach their ends.
All inputs are finite; a program needn't handle non-finite values.
Results may differ from the reference program's by a relative error of at most 0.001.
Values sent between devices are 32-bit elements; how exact they have to be, the bound alone decides.
A program may use at most 64 MiB of HBM per device.

```python
import jax
import jax.numpy as jnp
from jax import lax

D = 64
SUPPORT = 16384
ITERS = 2
CELLS = 16384
ATLASES = 4


def draw_cells(key, part):
    own_key = jax.random.fold_in(key, 1)
    values = jax.random.truncated_normal(own_key, -4.0, 4.0, (ATLASES, D, CELLS), jnp.float32)
    return values.astype(jnp.bfloat16)


def draw_support(key, part):
    own_key = jax.random.fold_in(key, 2)
    values = jax.random.truncated_normal(own_key, -4.0, 4.0, (D, SUPPORT), jnp.float32)
    return values.astype(jnp.bfloat16)


def setup_inputs(seed: int = 0) -> dict:
    seeds = jax.random.split(jax.random.key(seed), 3)
    cells = draw_cells(jax.random.fold_in(seeds[2], 71), 0)
    support = draw_support(jax.random.fold_in(seeds[2], 71), 0)
    return dict(cells=cells, support=support)


blur = 0.1


def reference(cells, support):
    dims = support.shape[0]
    total_support = support.shape[1]
    total_cells = cells.shape[2]
    atlases = cells.shape[0]
    width_block = min(512, total_support)
    count = total_support // width_block
    support_blocks = support.reshape(dims, count, width_block).transpose(1, 0, 2)
    squares_y = jnp.sum(jnp.square(support.astype(jnp.float32)), axis=0).reshape(count, width_block)
    duals_f = []
    duals_g = []
    summed = jnp.zeros((dims, total_support), jnp.float32)
    for atlas in range(atlases):
        points = cells[atlas]
        points_wide = points.astype(jnp.float32)
        squares_x = jnp.sum(jnp.square(points_wide), axis=0)

        def tile_cost(piece, near):
            cross = lax.dot_general(points, piece, (((0,), (0,)), ((), ())), preferred_element_type=jnp.float32)
            return (squares_x[:, None] + near[None, :] - 2.0 * cross) / dims

        dual_g = jnp.zeros((count, width_block), jnp.float32)
        dual_f = jnp.zeros((total_cells,), jnp.float32)
        for step in range(ITERS):
            def visit(carry, item):
                top, total = carry
                piece, near, gpart = item
                logits = (gpart[None, :] - tile_cost(piece, near)) / blur
                peak = jnp.maximum(top, jnp.max(logits, axis=1))
                total = total * jnp.exp(top - peak) + jnp.sum(jnp.exp(logits - peak[:, None]), axis=1)
                return (peak, total), None

            start_carry = (jnp.full((total_cells,), -jnp.inf, jnp.float32), jnp.zeros((total_cells,), jnp.float32))
            (top, total), unused = lax.scan(visit, start_carry, (support_blocks, squares_y, dual_g))
            dual_f = blur * jnp.log(1.0 / total_cells) - blur * (top + jnp.log(total))

            def column(item):
                piece, near = item
                logits = (dual_f[:, None] - tile_cost(piece, near)) / blur
                peak = jnp.max(logits, axis=0)
                mass = jnp.sum(jnp.exp(logits - peak[None, :]), axis=0)
                return blur * jnp.log(1.0 / total_support) - blur * (peak + jnp.log(mass))

            dual_g = lax.map(column, (support_blocks, squares_y))

        def weigh(item):
            piece, near, gpart = item
            plan = jnp.exp((dual_f[:, None] + gpart[None, :] - tile_cost(piece, near)) / blur)
            return jnp.dot(points_wide, plan, precision=lax.Precision.HIGHEST) * total_support

        terms = lax.map(weigh, (support_blocks, squares_y, dual_g))
        summed = summed + terms.transpose(1, 0, 2).reshape(dims, total_support)
        duals_f.append(dual_f)
        duals_g.append(dual_g.reshape(total_support))
    return jnp.stack(duals_f), jnp.stack(duals_g), summed / atlases
```

```python
import functools
import math

import jax
import jax.numpy as jnp
from jax import lax
from jax.experimental import pallas as pl
from jax.experimental.pallas import tpu as pltpu
from jax.sharding import Mesh
from jax.sharding import PartitionSpec as P

ITERS = 2
BLUR = 0.1
AXES = ("atlas", "row_0", "row_1", "col")
F32, BF16 = jnp.float32, jnp.bfloat16
LOW = -1e30
DEPTH = 128
GUARD = 16


def remote(src, dst, send, recv, device):
    return pltpu.make_async_remote_copy(
        src_ref=src,
        dst_ref=dst,
        send_sem=send,
        recv_sem=recv,
        device_id=device,
        device_id_type=pl.DeviceIdType.MESH,
    )


def three_rows(v, rows):
    hi = v.astype(BF16).astype(F32)
    rest = v - hi
    mid = rest.astype(BF16).astype(F32)
    low = rest - mid
    i = lax.broadcasted_iota(jnp.int32, (rows, v.shape[1]), 0)
    return jnp.where(i == 0, hi, jnp.where(i == 1, mid, jnp.where(i == 2, low, 0.0)))


def kernel(sizes, total_cells, total_support, *refs):
    (
        cells, support, out_f, out_g, out_n,
        xt_f, xt_g, yc, yf, half_y, gbuf, xt_all, xc_all, ycut,
        fx, gpart, gpair, gz, bfull, av, usend, urecv, tsend, ty, g2,
        f_s, f_r, gp_s, gp_r, gz_s, gz_r, gb_s, gb_r, av_s, av_r,
        ring_s, ring_r, u_s, u_r, ty_s, ty_r, g2_s, g2_r, g2p_s, g2p_r,
        nz_s, nz_r, ny_s, ny_r, np_s, np_r,
    ) = refs
    NY, NZ, NC, NX = sizes
    my, mz, mc, mx = (lax.axis_index(a) for a in AXES)
    dims, rows = cells.shape[1:]
    columns = support.shape[1]
    half = columns // NC
    part = dims // NY
    unit = dims * BLUR / 2.0
    scale = math.log2(math.e) / unit
    log_cells = unit * math.log(1.0 / total_cells)
    log_support = unit * math.log(1.0 / total_support)
    other = 1 - mc

    def at_z(k):
        return (my, lax.rem(mz + k, NZ), mc, mx)

    def at_y(k):
        return (lax.rem(my + k, NY), mz, mc, mx)

    def at_x(k):
        return (my, mz, mc, lax.rem(mx + k, NX))

    pair = (my, mz, other, mx)

    def from_z(k):
        return lax.rem(mz + NZ - k, NZ)

    def far_first(i):
        return NZ // 2 + (1 - 2 * lax.rem(i, 2)) * ((i + 1) // 2)

    def each(count, visit):
        def body(i, carry):
            visit(i)
            return carry

        lax.fori_loop(0, count, body, 0)

    barrier = pltpu.get_barrier_semaphore()

    def greet(device):
        pl.semaphore_signal(barrier, inc=1, device_id=device, device_id_type=pl.DeviceIdType.MESH)

    each(NZ - 1, lambda i: greet(at_z(far_first(i))))
    for k in range(1, NX):
        greet(at_x(k))
    for k in range(1, NY):
        greet(at_y(k))
    greet(pair)

    x32 = cells[0].astype(F32)
    gbuf[mz] = x32
    half_x = 0.5 * jnp.sum(x32 * x32, axis=0, keepdims=True)
    lane = lax.broadcasted_iota(jnp.int32, (128, DEPTH), 1)
    ones_lane = jnp.where((lane >= dims) & (lane < dims + 3), 1.0, 0.0)
    spare = jnp.zeros((DEPTH - dims, 128), F32)

    def turned(block):
        return jnp.transpose(jnp.concatenate([block, spare], axis=0))

    for r in range(0, rows, 128):
        t = turned(x32[:, r : r + 128])
        xt_g[r : r + 128, :] = t.astype(BF16)
        xt_f[r : r + 128, :] = (t + ones_lane).astype(BF16)
    step = 512

    def prepare(i):
        at = pl.ds(pl.multiple_of(i * step, step), step)
        y = support[:, at]
        yc[0:dims, at] = y
        yf[0:dims, at] = y
        i16 = lax.broadcasted_iota(jnp.int32, (GUARD, step), 0)
        yc[dims : dims + GUARD, at] = jnp.where(i16 < 3, 1.0, 0.0).astype(BF16)
        zeros = jnp.zeros((DEPTH - dims - GUARD, step), BF16)
        yc[dims + GUARD : DEPTH, at] = zeros
        yf[dims + GUARD : DEPTH, at] = zeros
        y32 = y.astype(F32)
        squares = 0.5 * jnp.sum(y32 * y32, axis=0, keepdims=True)
        half_y[:, at] = squares
        yf[dims : dims + GUARD, at] = three_rows(-squares, GUARD).astype(BF16)

    each(columns // step, prepare)

    def put_a(ref, a):
        ref[:, dims : dims + 8] = jnp.transpose(three_rows(a, 8)).astype(BF16)

    eye = lax.broadcasted_iota(jnp.int32, (128, 128), 0) == lax.broadcasted_iota(jnp.int32, (128, 128), 1)
    wide = 1024
    tall = min(256, rows)

    def f_pass(slot):
        def visit(r):
            at = pl.ds(pl.multiple_of(r * tall, tall), tall)
            xt = xt_f[at, :]
            top = jnp.full((tall, 128), LOW, F32)
            total = jnp.zeros((tall, 128), F32)
            for c in range(0, columns, wide):
                logits = jnp.dot(xt, yf[:, c : c + wide], preferred_element_type=F32)
                tiles = [logits[:, k : k + 128] for k in range(0, wide, 128)]
                peak = functools.reduce(jnp.maximum, tiles, top)
                total = total * jnp.exp2((top - peak) * scale)
                for tile in tiles:
                    total = total + jnp.exp2((tile - peak) * scale)
                top = peak
            peak = jnp.max(top, axis=1, keepdims=True)
            total = jnp.sum(total * jnp.exp2((top - peak) * scale), axis=1, keepdims=True)
            lse = peak + unit * jnp.log(total)
            for k in range(tall // 128):
                piece = jnp.where(eye, lse[k * 128 : (k + 1) * 128], 0.0)
                row = jnp.sum(piece, axis=0, keepdims=True)
                slot[:, pl.ds(pl.multiple_of(r * tall + k * 128, 128), 128)] = row

        each(rows // tall, visit)

    def g_pass():
        high = min(256, rows)

        def visit(i):
            w = yc[:, pl.ds(pl.multiple_of(i * step, step), step)]
            top = jnp.full((8, step), LOW, F32)
            total = jnp.zeros((8, step), F32)
            for r in range(0, rows, high):
                logits = jnp.dot(xt_g[r : r + high, :], w, preferred_element_type=F32)
                logits = logits.reshape(high // 8, 8, step)
                peak = jnp.maximum(top, jnp.max(logits, axis=0))
                total = total * jnp.exp2((top - peak) * scale) + jnp.sum(
                    jnp.exp2((logits - peak[None]) * scale), axis=0
                )
                top = peak
            peak = jnp.max(top, axis=0, keepdims=True)
            total = jnp.sum(total * jnp.exp2((top - peak) * scale), axis=0, keepdims=True)
            lse = peak + unit * jnp.log(total)
            for k in range(step // 128):
                r = i * (step // 128) + k
                gpart[r // NZ, pl.ds(lax.rem(r, NZ), 1), :] = lse[:, k * 128 : (k + 1) * 128]

        each(columns // step, visit)

    def merged(pieces):
        peak = functools.reduce(jnp.maximum, pieces)
        total = sum(jnp.exp2((piece - peak) * scale) for piece in pieces)
        return peak + unit * jnp.log(total)

    ahead, behind = NZ // 2, NZ // 2 - 1

    def right(s):
        slot = gbuf.at[from_z(s)]
        return remote(slot, slot, ring_s.at[0, s], ring_r.at[0, s], at_z(1))

    def left(s):
        slot = gbuf.at[lax.rem(mz + s, NZ)]
        return remote(slot, slot, ring_s.at[1, s], ring_r.at[1, s], at_z(NZ - 1))

    def spread(slot):
        block = gbuf[slot]
        xc_all[slot, 0:dims, :] = block.astype(BF16)
        i16 = lax.broadcasted_iota(jnp.int32, (GUARD, rows), 0)
        xc_all[slot, dims : dims + GUARD, :] = jnp.where(i16 < 1, 1.0, 0.0).astype(BF16)
        for r in range(0, rows, 128):
            xt_all[slot, r : r + 128, :] = turned(block[:, r : r + 128]).astype(BF16)

    def ring_step(s):
        if 0 < s <= ahead:
            right(s - 1).wait_recv()
        if s < ahead:
            right(s).start()
        if 0 < s <= behind:
            left(s - 1).wait_recv()
        if s < behind:
            left(s).start()

    def ring_spread(s):
        if s == 0:
            spread(mz)
        if 0 < s <= ahead:
            spread(from_z(s))
        if 0 < s <= behind:
            spread(lax.rem(mz + s, NZ))

    turns = list(range(ahead + 1))

    def turn():
        if turns:
            s = turns.pop(0)
            ring_step(s)
            ring_spread(s - 1)

    f_pass(fx.at[0, mx])
    pl.semaphore_wait(barrier, NX + NZ + NY - 2)

    def f_copy(it, k):
        slot = fx.at[it, mx]
        return remote(slot, slot, f_s.at[it, k - 1], f_r.at[it, k - 1], at_x(k))

    def z_copy(k):
        slot = gz.at[mz]
        return remote(slot, slot, gz_s.at[k], gz_r.at[k], at_z(k))

    def a_copy(k):
        slot = av.at[mz]
        return remote(slot, slot, av_s.at[k], av_r.at[k], at_z(k))

    def g2_copy(k):
        slot = g2.at[mc, mz]
        return remote(slot, slot, g2_s.at[k], g2_r.at[k], at_z(k))

    gp_copy = remote(gpart.at[other], gpair, gp_s, gp_r, pair)
    gb_copy = remote(bfull.at[mc], bfull.at[mc], gb_s, gb_r, pair)

    def f_exchange(it):
        for k in range(1, NX):
            f_copy(it, k).start()
        if it == 0:
            turn()
        for k in range(1, NX):
            f_copy(it, k).wait_recv()
        return log_cells - merged([fx[it, k] for k in range(NX)])

    a = f_exchange(0)
    put_a(xt_g, a)
    g_pass()
    gp_copy.start()
    gp_copy.wait_recv()
    gz[mz] = merged([gpart[mc], gpair[...]])
    each(NZ - 1, lambda i: z_copy(far_first(i)).start())
    turn()
    turn()
    each(NZ - 1, lambda i: z_copy(i + 1).wait_recv())
    bfull[mc] = log_support - merged([gz[k] for k in range(NZ)])
    gb_copy.start()
    turn()
    gb_copy.wait_recv()
    for h in range(NC):
        for r in range(NZ):
            j = (h * NZ + r) * 128
            yf[dims : dims + GUARD, j : j + 128] = three_rows(bfull[h, r : r + 1], GUARD).astype(BF16)
    f_pass(fx.at[1, mx])
    a = f_exchange(1)
    av[mz] = a
    out_f[...] = (a + half_x) * (2.0 / dims)
    each(NZ - 1, lambda i: a_copy(far_first(i)).start())
    while turns:
        turn()
    ring_spread(ahead)
    first = pl.ds(pl.multiple_of(mz * 128, 128), 128)
    second = pl.ds(pl.multiple_of(half + mz * 128, 128), 128)
    ycut[0] = yc[:, first]
    ycut[1] = yc[:, second]
    each(NZ - 1, lambda i: a_copy(i + 1).wait_recv())
    each(NZ, lambda k: put_a(xt_all.at[k], av[k]))

    weights = jnp.concatenate([ycut[0], ycut[1]], axis=1)

    def weigh(k, carry):
        top, total = carry
        logits = jnp.dot(xt_all[k], weights, preferred_element_type=F32)
        peak = jnp.maximum(top, jnp.max(logits, axis=0, keepdims=True))
        plan = jnp.exp2((logits - peak) * scale)
        hi = plan.astype(BF16)
        low = (plan - hi.astype(F32)).astype(BF16)
        xc = xc_all[k]
        total = (
            total * jnp.exp2((top - peak) * scale)
            + jnp.dot(xc, hi, preferred_element_type=F32)
            + jnp.dot(xc, low, preferred_element_type=F32)
        )
        return peak, total

    lines = dims + GUARD
    top, total = lax.fori_loop(
        0, NZ, weigh, (jnp.full((1, 256), LOW, F32), jnp.zeros((lines, 256), F32))
    )
    for h in range(NC):
        usend[h, 0:lines, :] = total[:, h * 128 : (h + 1) * 128]
        usend[h, lines : lines + 8, :] = jnp.broadcast_to(top[:, h * 128 : (h + 1) * 128], (8, 128))
    u_copy = remote(usend.at[other], urecv, u_s, u_r, pair)
    u_copy.start()
    u_copy.wait_recv()
    mine, theirs = usend[mc], urecv[...]
    peak = jnp.maximum(mine[lines : lines + 1], theirs[lines : lines + 1])
    total = mine[0:lines] * jnp.exp2((mine[lines : lines + 1] - peak) * scale) + theirs[
        0:lines
    ] * jnp.exp2((theirs[lines : lines + 1] - peak) * scale)
    mass = total[dims : dims + 1]
    tsend[...] = total[0:dims] / mass

    def t_copy(k):
        at = pl.ds(pl.multiple_of(lax.rem(my + k, NY) * part, part), part)
        return remote(tsend.at[at], ty.at[my], ty_s.at[k - 1], ty_r.at[k - 1], at_y(k))

    for k in range(1, NY):
        t_copy(k).start()
    g2[mc, mz] = log_support - peak - unit * jnp.log(mass)
    each(NZ - 1, lambda i: g2_copy(far_first(i)).start())
    band = pl.ds(pl.multiple_of(my * part, part), part)
    ty[my] = tsend[band, :]
    for k in range(1, NY):
        t_copy(k).wait_recv()

    def place(z):
        return out_n.at[band, pl.ds(pl.multiple_of(mc * half + z * 128, 128), 128)]

    place(mz)[...] = sum(ty[k] for k in range(NY)) * (1.0 / NY)

    def n_copy(k):
        return remote(place(mz), place(mz), nz_s.at[k], nz_r.at[k], at_z(k))

    each(NZ - 1, lambda i: n_copy(far_first(i)).start())

    def forward(z):
        for k in range(1, NY):
            remote(place(z), place(z), ny_s.at[k - 1], ny_r.at[k - 1], at_y(k)).start()

    forward(mz)

    def arrived(i):
        k = far_first(NZ - 2 - i)
        n_copy(k).wait_recv()
        forward(from_z(k))

    each(NZ - 1, arrived)
    own_half = pl.ds(pl.multiple_of(mc * half, half), half)

    def strip(y):
        return out_n.at[pl.ds(pl.multiple_of(y * part, part), part), own_half]

    def np_copy(k):
        piece = strip(lax.rem(my + NY - k, NY))
        return remote(piece, piece, np_s.at[k], np_r.at[k], pair)

    np_copy(0).start()
    each(NZ - 1, lambda i: g2_copy(i + 1).wait_recv())
    g2p_copy = remote(g2.at[mc], g2.at[mc], g2p_s, g2p_r, pair)
    g2p_copy.start()

    def ny_whole(k):
        piece = strip(lax.rem(my + NY - k, NY))
        return remote(piece, piece, ny_s.at[k - 1], ny_r.at[k - 1], at_y(k))

    for k in range(1, NY):
        ny_whole(k).wait_recv()
        np_copy(k).start()
    g2p_copy.wait_recv()
    for h in range(NC):
        for r in range(NZ):
            at = slice((h * NZ + r) * 128, (h * NZ + r + 1) * 128)
            out_g[:, at] = (g2[h, r] + half_y[:, at]) * (2.0 / dims)
    for k in range(NY):
        np_copy(k).wait_recv()

    for it in range(ITERS):
        for k in range(1, NX):
            f_copy(it, k).wait_send()
    gp_copy.wait_send()
    gb_copy.wait_send()
    u_copy.wait_send()
    g2p_copy.wait_send()
    for k in range(1, NY):
        t_copy(k).wait_send()
        ny_whole(k).wait_send()
    for k in range(NY):
        np_copy(k).wait_send()
    for s in range(ahead):
        right(s).wait_send()
    for s in range(behind):
        left(s).wait_send()

    def left_z(i):
        for copy in (z_copy, a_copy, g2_copy, n_copy):
            copy(i + 1).wait_send()

    each(NZ - 1, left_z)


def solution(mesh):
    NY, NX = mesh.shape["atlas"], mesh.shape["col"]
    NC = 2
    NZ = mesh.shape["row"] // NC
    split = Mesh(mesh.devices.reshape(NY, NZ, NC, NX), AXES)
    dma = pltpu.SemaphoreType.DMA

    def shards(cells, support):
        dims, rows = cells.shape[1:]
        columns = support.shape[1]
        part = dims // NY
        lines = dims + GUARD
        vmem = pltpu.VMEM
        scratch = [
            vmem((rows, DEPTH), BF16),
            vmem((rows, DEPTH), BF16),
            vmem((DEPTH, columns), BF16),
            vmem((DEPTH, columns), BF16),
            vmem((1, columns), F32),
            vmem((NZ, dims, rows), F32),
            vmem((NZ, rows, DEPTH), BF16),
            vmem((NZ, lines, rows), BF16),
            vmem((NC, DEPTH, 128), BF16),
            vmem((ITERS, NX, 1, rows), F32),
            vmem((NC, NZ, 128), F32),
            vmem((NZ, 128), F32),
            vmem((NZ, NZ, 128), F32),
            vmem((NC, NZ, 128), F32),
            vmem((NZ, 1, rows), F32),
            vmem((NC, lines + 8, 128), F32),
            vmem((lines + 8, 128), F32),
            vmem((dims, 128), F32),
            vmem((NY, part, 128), F32),
            vmem((NC, NZ, 1, 128), F32),
            dma((ITERS, NX - 1)), dma((ITERS, NX - 1)),
            dma, dma,
            dma((NZ,)), dma((NZ,)),
            dma, dma,
            dma((NZ,)), dma((NZ,)),
            dma((2, NZ // 2)), dma((2, NZ // 2)),
            dma, dma,
            dma((NY - 1,)), dma((NY - 1,)),
            dma((NZ,)), dma((NZ,)),
            dma, dma,
            dma((NZ,)), dma((NZ,)),
            dma((NY - 1,)), dma((NY - 1,)),
            dma((NY,)), dma((NY,)),
        ]
        body = functools.partial(kernel, (NY, NZ, NC, NX), rows * NZ * NC, columns * NX)
        return pl.pallas_call(
            body,
            out_shape=(
                jax.ShapeDtypeStruct((1, rows), F32),
                jax.ShapeDtypeStruct((1, columns), F32),
                jax.ShapeDtypeStruct((dims, columns), F32),
            ),
            in_specs=[pl.BlockSpec(memory_space=pltpu.VMEM)] * 2,
            out_specs=[pl.BlockSpec(memory_space=pltpu.VMEM)] * 3,
            scratch_shapes=scratch,
            compiler_params=pltpu.CompilerParams(
                collective_id=0, has_side_effects=True, vmem_limit_bytes=56 << 20
            ),
        )(cells, support)

    row = ("row_0", "row_1")
    in_specs = (P("atlas", None, row), P(None, "col"))
    out_specs = (P("atlas", row), P("atlas", "col"), P(None, "col"))
    return jax.shard_map(shards, mesh=split, in_specs=in_specs, out_specs=out_specs, check_vma=False)
```

```python
import functools
import math

import jax
import jax.numpy as jnp
from jax import lax
from jax.experimental import pallas as pl
from jax.experimental.pallas import tpu as pltpu
from jax.sharding import Mesh
from jax.sharding import PartitionSpec as P

ITERS = 2
BLUR = 0.1
AXES = ("atlas", "row_0", "row_1", "col")
F32, BF16 = jnp.float32, jnp.bfloat16
LOW = -1e30
DEPTH = 128
GUARD = 16
CHUNKS = 2
GROUP = 4


def remote(src, dst, send, recv, device):
    return pltpu.make_async_remote_copy(
        src_ref=src,
        dst_ref=dst,
        send_sem=send,
        recv_sem=recv,
        device_id=device,
        device_id_type=pl.DeviceIdType.MESH,
    )


def three_rows(v, rows):
    hi = v.astype(BF16).astype(F32)
    rest = v - hi
    mid = rest.astype(BF16).astype(F32)
    low = rest - mid
    i = lax.broadcasted_iota(jnp.int32, (rows, v.shape[1]), 0)
    return jnp.where(i == 0, hi, jnp.where(i == 1, mid, jnp.where(i == 2, low, 0.0)))


def kernel(sizes, total_cells, total_support, *refs):
    (
        cells, support, out_f, out_g, out_n,
        xt_f, xt_g, yc, yf, half_y, gbuf, xg_all, y_own,
        fx, gpart, gpair, gz, bfull, av, usend, urecv, tsend, ty, g2,
        f_s, f_r, gp_s, gp_r, gz_s, gz_r, gb_s, gb_r, av_s, av_r,
        ring_s, ring_r, u_s, u_r, ty_s, ty_r, g2_s, g2_r, g2p_s, g2p_r,
        nz_s, nz_r, ny_s, ny_r, np_s, np_r,
    ) = refs
    NY, NZ, NC, NX = sizes
    my, mz, mc, mx = (lax.axis_index(a) for a in AXES)
    dims, rows = cells.shape[1:]
    columns = support.shape[1]
    half = columns // NC
    part = dims // NY
    unit = dims * BLUR / 2.0
    scale = math.log2(math.e) / unit
    log_cells = unit * math.log(1.0 / total_cells)
    log_support = unit * math.log(1.0 / total_support)
    other = 1 - mc

    def at_z(k):
        return (my, lax.rem(mz + k, NZ), mc, mx)

    def at_y(k):
        return (lax.rem(my + k, NY), mz, mc, mx)

    def at_x(k):
        return (my, mz, mc, lax.rem(mx + k, NX))

    pair = (my, mz, other, mx)

    def from_z(k):
        return lax.rem(mz + NZ - k, NZ)

    def far_first(i):
        return NZ // 2 + (1 - 2 * lax.rem(i, 2)) * ((i + 1) // 2)

    def each(count, visit):
        def body(i, carry):
            visit(i)
            return carry

        lax.fori_loop(0, count, body, 0)

    barrier = pltpu.get_barrier_semaphore()

    def greet(device):
        pl.semaphore_signal(barrier, inc=1, device_id=device, device_id_type=pl.DeviceIdType.MESH)

    each(NZ - 1, lambda i: greet(at_z(far_first(i))))
    for k in range(1, NX):
        greet(at_x(k))
    for k in range(1, NY):
        greet(at_y(k))
    greet(pair)

    x32 = cells[0].astype(F32)
    gbuf[mz] = x32
    half_x = 0.5 * jnp.sum(x32 * x32, axis=0, keepdims=True)
    lane = lax.broadcasted_iota(jnp.int32, (128, DEPTH), 1)
    ones_lane = jnp.where((lane >= dims) & (lane < dims + 3), 1.0, 0.0)
    spare = jnp.zeros((DEPTH - dims, 128), F32)

    def turned(block):
        return jnp.transpose(jnp.concatenate([block, spare], axis=0))

    for r in range(0, rows, 128):
        t = turned(x32[:, r : r + 128])
        xt_g[r : r + 128, :] = t.astype(BF16)
        xt_f[r : r + 128, :] = (t + ones_lane).astype(BF16)
    step = 512
    for p in range(NZ):
        xg_all[p, dims + GUARD : DEPTH, :] = jnp.zeros((DEPTH - dims - GUARD, rows), BF16)

    def prepare(i):
        at = pl.ds(pl.multiple_of(i * step, step), step)
        y = support[:, at]
        yc[0:dims, at] = y
        yf[0:dims, at] = y
        i16 = lax.broadcasted_iota(jnp.int32, (GUARD, step), 0)
        yc[dims : dims + GUARD, at] = jnp.where(i16 < 3, 1.0, 0.0).astype(BF16)
        zeros = jnp.zeros((DEPTH - dims - GUARD, step), BF16)
        yc[dims + GUARD : DEPTH, at] = zeros
        yf[dims + GUARD : DEPTH, at] = zeros
        y32 = y.astype(F32)
        squares = 0.5 * jnp.sum(y32 * y32, axis=0, keepdims=True)
        half_y[:, at] = squares
        yf[dims : dims + GUARD, at] = three_rows(-squares, GUARD).astype(BF16)

    each(columns // step, prepare)

    def put_a(ref, a):
        ref[:, dims : dims + 8] = jnp.transpose(three_rows(a, 8)).astype(BF16)

    eye = lax.broadcasted_iota(jnp.int32, (128, 128), 0) == lax.broadcasted_iota(jnp.int32, (128, 128), 1)
    wide = 1024
    tall = min(256, rows)

    def f_pass(slot, first, last):
        def visit(r):
            r = r + first
            at = pl.ds(pl.multiple_of(r * tall, tall), tall)
            xt = xt_f[at, :]
            top = jnp.full((tall, 128), LOW, F32)
            total = jnp.zeros((tall, 128), F32)
            for c in range(0, columns, wide):
                logits = jnp.dot(xt, yf[:, c : c + wide], preferred_element_type=F32)
                tiles = [logits[:, k : k + 128] for k in range(0, wide, 128)]
                peak = functools.reduce(jnp.maximum, tiles, top)
                total = total * jnp.exp2((top - peak) * scale)
                for tile in tiles:
                    total = total + jnp.exp2((tile - peak) * scale)
                top = peak
            peak = jnp.max(top, axis=1, keepdims=True)
            total = jnp.sum(total * jnp.exp2((top - peak) * scale), axis=1, keepdims=True)
            lse = peak + unit * jnp.log(total)
            for k in range(tall // 128):
                piece = jnp.where(eye, lse[k * 128 : (k + 1) * 128], 0.0)
                row = jnp.sum(piece, axis=0, keepdims=True)
                slot[:, pl.ds(pl.multiple_of(r * tall + k * 128, 128), 128)] = row

        each(last - first, visit)

    def g_pass(first, last):
        high = min(256, rows)

        def visit(i):
            i = i + first
            w = yc[:, pl.ds(pl.multiple_of(i * step, step), step)]
            top = jnp.full((8, step), LOW, F32)
            total = jnp.zeros((8, step), F32)
            for r in range(0, rows, high):
                logits = jnp.dot(xt_g[r : r + high, :], w, preferred_element_type=F32)
                logits = logits.reshape(high // 8, 8, step)
                peak = jnp.maximum(top, jnp.max(logits, axis=0))
                total = total * jnp.exp2((top - peak) * scale) + jnp.sum(
                    jnp.exp2((logits - peak[None]) * scale), axis=0
                )
                top = peak
            peak = jnp.max(top, axis=0, keepdims=True)
            total = jnp.sum(total * jnp.exp2((top - peak) * scale), axis=0, keepdims=True)
            lse = peak + unit * jnp.log(total)
            for k in range(step // 128):
                r = i * (step // 128) + k
                gpart[r // NZ, pl.ds(lax.rem(r, NZ), 1), :] = lse[:, k * 128 : (k + 1) * 128]

        each(last - first, visit)

    def merged(pieces):
        peak = functools.reduce(jnp.maximum, pieces)
        total = sum(jnp.exp2((piece - peak) * scale) for piece in pieces)
        return peak + unit * jnp.log(total)

    ahead, behind = NZ // 2, NZ // 2 - 1

    piece_dims = dims // CHUNKS

    def ring_copy(direction, source, s, h, device):
        piece = gbuf.at[source, pl.ds(h * piece_dims, piece_dims)]
        return remote(piece, piece, ring_s.at[direction, s, h], ring_r.at[direction, s, h], device)

    def right(s, h):
        return ring_copy(0, from_z(s), s, h, at_z(1))

    def left(s, h):
        return ring_copy(1, lax.rem(mz + s, NZ), s, h, at_z(NZ - 1))

    def source_of(p):
        s = (p + 1) // 2
        return from_z(s) if p % 2 else lax.rem(mz + s, NZ)

    def spread(p):
        xg_all[p, 0:dims, :] = gbuf[source_of(p)].astype(BF16)

    turns = [(s, h) for s in range(ahead + 1) for h in range(CHUNKS)]

    def turn(count=1):
        for _ in range(min(count, len(turns))):
            s, h = turns.pop(0)
            if 0 < s <= ahead:
                right(s - 1, h).wait_recv()
            if s < ahead:
                right(s, h).start()
            if 0 < s <= behind:
                left(s - 1, h).wait_recv()
            if s < behind:
                left(s, h).start()
            if h == CHUNKS - 1:
                if s == 0:
                    spread(0)
                if 0 < s <= ahead:
                    spread(2 * s - 1)
                if 0 < s <= behind:
                    spread(2 * s)

    f_pass(fx.at[0, mx], 0, rows // tall)
    pl.semaphore_wait(barrier, NX + NZ + NY - 2)

    def f_copy(it, k):
        slot = fx.at[it, mx]
        return remote(slot, slot, f_s.at[it, k - 1], f_r.at[it, k - 1], at_x(k))

    def z_copy(k):
        slot = gz.at[mz]
        return remote(slot, slot, gz_s.at[k], gz_r.at[k], at_z(k))

    def a_copy(k):
        slot = av.at[mz]
        return remote(slot, slot, av_s.at[k], av_r.at[k], at_z(k))

    def g2_copy(k):
        slot = g2.at[mc, mz]
        return remote(slot, slot, g2_s.at[k], g2_r.at[k], at_z(k))

    gp_copy = remote(gpart.at[other], gpair, gp_s, gp_r, pair)
    gb_copy = remote(bfull.at[mc], bfull.at[mc], gb_s, gb_r, pair)

    def f_exchange(it):
        for k in range(1, NX):
            f_copy(it, k).start()
        turn(2)
        for k in range(1, NX):
            f_copy(it, k).wait_recv()
        return log_cells - merged([fx[it, k] for k in range(NX)])

    a = f_exchange(0)
    put_a(xt_g, a)
    count = columns // step
    g_pass(0, count // 2)
    turn()
    g_pass(count // 2, count)
    gp_copy.start()
    turn()
    gp_copy.wait_recv()
    gz[mz] = merged([gpart[mc], gpair[...]])
    each(NZ - 1, lambda i: z_copy(far_first(i)).start())
    turn(5)
    each(NZ - 1, lambda i: z_copy(i + 1).wait_recv())
    bfull[mc] = log_support - merged([gz[k] for k in range(NZ)])
    gb_copy.start()
    gb_copy.wait_recv()
    for h in range(NC):
        for r in range(NZ):
            j = (h * NZ + r) * 128
            yf[dims : dims + GUARD, j : j + 128] = three_rows(bfull[h, r : r + 1], GUARD).astype(BF16)
    turn()
    f_pass(fx.at[1, mx], 0, 1)
    turn()
    f_pass(fx.at[1, mx], 1, rows // tall)
    a = f_exchange(1)
    av[mz] = a
    out_f[...] = (a + half_x) * (2.0 / dims)
    each(NZ - 1, lambda i: a_copy(far_first(i)).start())
    for h in range(NC):
        at = pl.ds(pl.multiple_of(h * half + mz * 128, 128), 128)
        y_own[h * 128 : (h + 1) * 128, :] = jnp.transpose(yc[:, at].astype(F32)).astype(BF16)
    turn(4)
    each(NZ - 1, lambda i: a_copy(i + 1).wait_recv())

    def weigh(first, carry):
        top, total = carry
        weights = y_own[...]
        products, blocks = [], []
        for p in range(first, first + GROUP):
            rows16 = three_rows(av[source_of(p)], GUARD)
            i16 = lax.broadcasted_iota(jnp.int32, rows16.shape, 0)
            xg_all[p, dims : dims + GUARD, :] = jnp.where(i16 == 3, 1.0, rows16).astype(BF16)
            blocks.append(xg_all[p])
            products.append(jnp.dot(weights, blocks[-1], preferred_element_type=F32))
        tiles = [x[:, k : k + 128] for x in products for k in range(0, rows, 128)]
        peak = jnp.max(functools.reduce(jnp.maximum, tiles), axis=1, keepdims=True)
        peak = jnp.maximum(top, peak)
        total = total * jnp.exp2((top - peak) * scale)
        for logits, block in zip(products, blocks):
            plan = jnp.exp2((logits - peak) * scale)
            hi = plan.astype(BF16)
            low = (plan - hi.astype(F32)).astype(BF16)
            for half_plan in (hi, low):
                total = total + lax.dot_general(
                    half_plan, block, (((1,), (1,)), ((), ())), preferred_element_type=F32
                )
        return peak, total

    wide_j = NC * 128
    carry = jnp.full((wide_j, 1), LOW, F32), jnp.zeros((wide_j, DEPTH), F32)
    for first in range(0, NZ, GROUP):
        while turns and turns[0][0] <= (first + GROUP) // 2:
            turn()
        carry = weigh(first, carry)
    top, total = carry
    row_mass, row_top, lines = dims + 3, dims + 4, dims + 8
    lane_u = lax.broadcasted_iota(jnp.int32, (wide_j, DEPTH), 1)
    total = jnp.where(lane_u == row_top, top, total)
    for h in range(NC):
        usend[h] = jnp.transpose(total[h * 128 : (h + 1) * 128])[0:lines]
    u_copy = remote(usend.at[other], urecv, u_s, u_r, pair)
    u_copy.start()
    u_copy.wait_recv()
    mine, theirs = usend[mc], urecv[...]
    top_one, top_two = mine[row_top : row_top + 1], theirs[row_top : row_top + 1]
    peak = jnp.maximum(top_one, top_two)
    total = mine * jnp.exp2((top_one - peak) * scale) + theirs * jnp.exp2((top_two - peak) * scale)
    mass = total[row_mass : row_mass + 1]
    tsend[...] = total[0:dims] / mass

    def t_copy(k):
        at = pl.ds(pl.multiple_of(lax.rem(my + k, NY) * part, part), part)
        return remote(tsend.at[at], ty.at[my], ty_s.at[k - 1], ty_r.at[k - 1], at_y(k))

    for k in range(1, NY):
        t_copy(k).start()
    g2[mc, mz] = log_support - peak - unit * jnp.log(mass)
    each(NZ - 1, lambda i: g2_copy(far_first(i)).start())
    band = pl.ds(pl.multiple_of(my * part, part), part)
    ty[my] = tsend[band, :]
    for k in range(1, NY):
        t_copy(k).wait_recv()

    def place(z):
        return out_n.at[band, pl.ds(pl.multiple_of(mc * half + z * 128, 128), 128)]

    place(mz)[...] = sum(ty[k] for k in range(NY)) * (1.0 / NY)

    def n_copy(k):
        return remote(place(mz), place(mz), nz_s.at[k], nz_r.at[k], at_z(k))

    each(NZ - 1, lambda i: n_copy(far_first(i)).start())

    def forward(z):
        for k in range(1, NY):
            remote(place(z), place(z), ny_s.at[k - 1], ny_r.at[k - 1], at_y(k)).start()

    forward(mz)

    def arrived(i):
        k = far_first(NZ - 2 - i)
        n_copy(k).wait_recv()
        forward(from_z(k))

    each(NZ - 1, arrived)
    own_half = pl.ds(pl.multiple_of(mc * half, half), half)

    def strip(y):
        return out_n.at[pl.ds(pl.multiple_of(y * part, part), part), own_half]

    def np_copy(k):
        piece = strip(lax.rem(my + NY - k, NY))
        return remote(piece, piece, np_s.at[k], np_r.at[k], pair)

    np_copy(0).start()
    each(NZ - 1, lambda i: g2_copy(i + 1).wait_recv())
    g2p_copy = remote(g2.at[mc], g2.at[mc], g2p_s, g2p_r, pair)
    g2p_copy.start()

    def ny_whole(k):
        piece = strip(lax.rem(my + NY - k, NY))
        return remote(piece, piece, ny_s.at[k - 1], ny_r.at[k - 1], at_y(k))

    for k in range(1, NY):
        ny_whole(k).wait_recv()
        np_copy(k).start()
    g2p_copy.wait_recv()
    for h in range(NC):
        for r in range(NZ):
            at = slice((h * NZ + r) * 128, (h * NZ + r + 1) * 128)
            out_g[:, at] = (g2[h, r] + half_y[:, at]) * (2.0 / dims)
    for k in range(NY):
        np_copy(k).wait_recv()

    for it in range(ITERS):
        for k in range(1, NX):
            f_copy(it, k).wait_send()
    gp_copy.wait_send()
    gb_copy.wait_send()
    u_copy.wait_send()
    g2p_copy.wait_send()
    for k in range(1, NY):
        t_copy(k).wait_send()
        ny_whole(k).wait_send()
    for k in range(NY):
        np_copy(k).wait_send()
    for h in range(CHUNKS):
        for s in range(ahead):
            right(s, h).wait_send()
        for s in range(behind):
            left(s, h).wait_send()

    def left_z(i):
        for copy in (z_copy, a_copy, g2_copy, n_copy):
            copy(i + 1).wait_send()

    each(NZ - 1, left_z)


def handed_on(*refs):
    arrays, results, held, done = refs[:3], refs[3:6], refs[6:9], refs[9]
    pieces = []
    for array, hold, result in zip(arrays, held, results):
        lines = array.shape[0]
        for at in range(0, lines, 16):
            piece = slice(at, min(at + 16, lines))
            pieces.append((array.at[piece], hold.at[piece], result.at[piece]))
    pieces = pieces[2:] + pieces[:2]
    inward = [pltpu.make_async_copy(p[0], p[1], done.at[0, k]) for k, p in enumerate(pieces)]
    outward = [pltpu.make_async_copy(p[1], p[2], done.at[1, k]) for k, p in enumerate(pieces)]
    for copy in inward:
        copy.start()
    for before, after in zip(inward, outward):
        before.wait()
        after.start()
    for copy in outward:
        copy.wait()


def solution(mesh):
    NY, NX = mesh.shape["atlas"], mesh.shape["col"]
    NC = 2
    NZ = mesh.shape["row"] // NC
    split = Mesh(mesh.devices.reshape(NY, NZ, NC, NX), AXES)
    dma = pltpu.SemaphoreType.DMA

    def shards(cells, support):
        dims, rows = cells.shape[1:]
        columns = support.shape[1]
        part = dims // NY
        lines = dims + 8
        vmem = pltpu.VMEM
        scratch = [
            vmem((rows, DEPTH), BF16),
            vmem((rows, DEPTH), BF16),
            vmem((DEPTH, columns), BF16),
            vmem((DEPTH, columns), BF16),
            vmem((1, columns), F32),
            vmem((NZ, dims, rows), F32),
            vmem((NZ, DEPTH, rows), BF16),
            vmem((NC * 128, DEPTH), BF16),
            vmem((ITERS, NX, 1, rows), F32),
            vmem((NC, NZ, 128), F32),
            vmem((NZ, 128), F32),
            vmem((NZ, NZ, 128), F32),
            vmem((NC, NZ, 128), F32),
            vmem((NZ, 1, rows), F32),
            vmem((NC, lines, 128), F32),
            vmem((lines, 128), F32),
            vmem((dims, 128), F32),
            vmem((NY, part, 128), F32),
            vmem((NC, NZ, 1, 128), F32),
            dma((ITERS, NX - 1)), dma((ITERS, NX - 1)),
            dma, dma,
            dma((NZ,)), dma((NZ,)),
            dma, dma,
            dma((NZ,)), dma((NZ,)),
            dma((2, NZ // 2, CHUNKS)), dma((2, NZ // 2, CHUNKS)),
            dma, dma,
            dma((NY - 1,)), dma((NY - 1,)),
            dma((NZ,)), dma((NZ,)),
            dma, dma,
            dma((NZ,)), dma((NZ,)),
            dma((NY - 1,)), dma((NY - 1,)),
            dma((NY,)), dma((NY,)),
        ]
        body = functools.partial(kernel, (NY, NZ, NC, NX), rows * NZ * NC, columns * NX)
        shapes = (
            jax.ShapeDtypeStruct((1, rows), F32),
            jax.ShapeDtypeStruct((1, columns), F32),
            jax.ShapeDtypeStruct((dims, columns), F32),
        )
        found = pl.pallas_call(
            body,
            out_shape=shapes,
            in_specs=[pl.BlockSpec(memory_space=pltpu.VMEM)] * 2,
            out_specs=[pl.BlockSpec(memory_space=pltpu.VMEM)] * 3,
            scratch_shapes=scratch,
            compiler_params=pltpu.CompilerParams(
                collective_id=0, has_side_effects=True, vmem_limit_bytes=56 << 20
            ),
        )(cells, support)
        return pl.pallas_call(
            handed_on,
            out_shape=shapes,
            in_specs=[pl.BlockSpec(memory_space=pl.ANY)] * 3,
            out_specs=[pl.BlockSpec(memory_space=pl.ANY)] * 3,
            scratch_shapes=[vmem(shape.shape, F32) for shape in shapes] + [dma((2, 2 + dims // 16))],
        )(*found)

    row = ("row_0", "row_1")
    in_specs = (P("atlas", None, row), P(None, "col"))
    out_specs = (P("atlas", row), P("atlas", "col"), P(None, "col"))
    return jax.shard_map(shards, mesh=split, in_specs=in_specs, out_specs=out_specs, check_vma=False)
```

```python
import functools
import math

import jax
import jax.numpy as jnp
from jax import lax
from jax.experimental import pallas as pl
from jax.experimental.pallas import tpu as pltpu
from jax.sharding import Mesh
from jax.sharding import PartitionSpec as P

ITERS = 2
BLUR = 0.1
AXES = ("atlas", "row_0", "row_1", "col")
F32, BF16 = jnp.float32, jnp.bfloat16
LOW = -1e30
DEPTH = 128
GUARD = 16
GZ = 6
AV = 4
CHUNKS = 2
SHARERS = 2
GROUP = 4


def remote(src, dst, send, recv, device):
    return pltpu.make_async_remote_copy(
        src_ref=src,
        dst_ref=dst,
        send_sem=send,
        recv_sem=recv,
        device_id=device,
        device_id_type=pl.DeviceIdType.MESH,
    )


def three_rows(v, rows):
    hi = v.astype(BF16).astype(F32)
    rest = v - hi
    mid = rest.astype(BF16).astype(F32)
    low = rest - mid
    i = lax.broadcasted_iota(jnp.int32, (rows, v.shape[1]), 0)
    return jnp.where(i == 0, hi, jnp.where(i == 1, mid, jnp.where(i == 2, low, 0.0)))


def kernel(sizes, total_cells, total_support, *refs):
    (
        cells_in, support_in, out_f, out_g, out_n, cells, support, in_sem,
        xt_f, xt_g, yc, yf, half_y, gbuf, xg_all, y_own,
        fx, gpart, gpair, gz, bfull, av, usend, urecv, tsend, ty, g2,
        f_s, f_r, gp_s, gp_r, gz_s, gz_r, gb_s, gb_r, av_s, av_r,
        ring_s, ring_r, share_s, share_r, u_s, u_r, ty_s, ty_r, g2_s, g2_r, g2p_s, g2p_r,
        nz_s, nz_r, ny_s, ny_r, np_s, np_r,
    ) = refs
    NY, NZ, NC, NX = sizes
    my, mz, mc, mx = (lax.axis_index(a) for a in AXES)
    dims, rows = cells_in.shape[1:]
    columns = support_in.shape[1]
    half = columns // NC
    part = dims // NY
    unit = dims * BLUR / 2.0
    scale = math.log2(math.e) / unit
    log_cells = unit * math.log(1.0 / total_cells)
    log_support = unit * math.log(1.0 / total_support)
    other = 1 - mc

    def at_z(k):
        return (my, lax.rem(mz + k, NZ), mc, mx)

    def at_y(k):
        return (lax.rem(my + k, NY), mz, mc, mx)

    def at_x(k):
        return (my, mz, mc, lax.rem(mx + k, NX))

    pair = (my, mz, other, mx)

    def from_z(k):
        return lax.rem(mz + NZ - k, NZ)

    def far_first(i):
        return NZ // 2 + (1 - 2 * lax.rem(i, 2)) * ((i + 1) // 2)

    def each(count, visit):
        def body(i, carry):
            visit(i)
            return carry

        lax.fori_loop(0, count, body, 0)

    barrier = pltpu.get_barrier_semaphore()

    def greet(device):
        pl.semaphore_signal(barrier, inc=1, device_id=device, device_id_type=pl.DeviceIdType.MESH)

    loads = [
        pltpu.make_async_copy(cells_in, cells, in_sem.at[0]),
        pltpu.make_async_copy(support_in, support, in_sem.at[1]),
    ]
    for load in loads:
        load.start()
    each(NZ - 1, lambda i: greet(at_z(far_first(i))))
    for k in range(1, NX):
        greet(at_x(k))
    for k in range(1, NY):
        greet(at_y(k))
    greet(pair)

    loads[0].wait()
    x32 = cells[0].astype(F32)
    gbuf[mz] = x32
    half_x = 0.5 * jnp.sum(x32 * x32, axis=0, keepdims=True)
    lane = lax.broadcasted_iota(jnp.int32, (128, DEPTH), 1)
    ones_lane = jnp.where((lane >= dims) & (lane < dims + 3), 1.0, 0.0)
    spare = jnp.zeros((DEPTH - dims, 128), F32)

    def turned(block):
        return jnp.transpose(jnp.concatenate([block, spare], axis=0))

    for r in range(0, rows, 128):
        t = turned(x32[:, r : r + 128])
        xt_g[r : r + 128, :] = t.astype(BF16)
        xt_f[r : r + 128, :] = (t + ones_lane).astype(BF16)
    step = 512
    for p in range(NZ):
        xg_all[p, dims + GUARD : DEPTH, :] = jnp.zeros((DEPTH - dims - GUARD, rows), BF16)

    def prepare(i):
        at = pl.ds(pl.multiple_of(i * step, step), step)
        y = support[:, at]
        yc[0:dims, at] = y
        yf[0:dims, at] = y
        i16 = lax.broadcasted_iota(jnp.int32, (GUARD, step), 0)
        yc[dims : dims + GUARD, at] = jnp.where(i16 < 3, 1.0, 0.0).astype(BF16)
        zeros = jnp.zeros((DEPTH - dims - GUARD, step), BF16)
        yc[dims + GUARD : DEPTH, at] = zeros
        yf[dims + GUARD : DEPTH, at] = zeros
        y32 = y.astype(F32)
        squares = 0.5 * jnp.sum(y32 * y32, axis=0, keepdims=True)
        half_y[:, at] = squares
        yf[dims : dims + GUARD, at] = three_rows(-squares, GUARD).astype(BF16)

    loads[1].wait()
    each(columns // step, prepare)

    def put_a(ref, a):
        ref[:, dims : dims + 8] = jnp.transpose(three_rows(a, 8)).astype(BF16)

    eye = lax.broadcasted_iota(jnp.int32, (128, 128), 0) == lax.broadcasted_iota(jnp.int32, (128, 128), 1)
    wide = 1024
    tall = min(256, rows)

    def f_pass(slot, first, last):
        def visit(r):
            r = r + first
            at = pl.ds(pl.multiple_of(r * tall, tall), tall)
            xt = xt_f[at, :]
            top = jnp.full((tall, 128), LOW, F32)
            total = jnp.zeros((tall, 128), F32)
            for c in range(0, columns, wide):
                logits = jnp.dot(xt, yf[:, c : c + wide], preferred_element_type=F32)
                tiles = [logits[:, k : k + 128] for k in range(0, wide, 128)]
                peak = functools.reduce(jnp.maximum, tiles, top)
                total = total * jnp.exp2((top - peak) * scale)
                for tile in tiles:
                    total = total + jnp.exp2((tile - peak) * scale)
                top = peak
            peak = jnp.max(top, axis=1, keepdims=True)
            total = jnp.sum(total * jnp.exp2((top - peak) * scale), axis=1, keepdims=True)
            lse = peak + unit * jnp.log(total)
            for k in range(tall // 128):
                piece = jnp.where(eye, lse[k * 128 : (k + 1) * 128], 0.0)
                row = jnp.sum(piece, axis=0, keepdims=True)
                slot[:, pl.ds(pl.multiple_of(r * tall + k * 128, 128), 128)] = row

        each(last - first, visit)

    def g_pass(first, last):
        high = min(256, rows)

        for i in range(first, last):
            w = yc[:, i * step : (i + 1) * step]
            top = jnp.full((8, step), LOW, F32)
            total = jnp.zeros((8, step), F32)
            for r in range(0, rows, high):
                logits = jnp.dot(xt_g[r : r + high, :], w, preferred_element_type=F32)
                logits = logits.reshape(high // 8, 8, step)
                peak = jnp.maximum(top, jnp.max(logits, axis=0))
                total = total * jnp.exp2((top - peak) * scale) + jnp.sum(
                    jnp.exp2((logits - peak[None]) * scale), axis=0
                )
                top = peak
            peak = jnp.max(top, axis=0, keepdims=True)
            total = jnp.sum(total * jnp.exp2((top - peak) * scale), axis=0, keepdims=True)
            lse = peak + unit * jnp.log(total)
            for k in range(step // 128):
                r = i * (step // 128) + k
                gpart[r // NZ, r % NZ : r % NZ + 1, :] = lse[:, k * 128 : (k + 1) * 128]

    def merged(pieces):
        peak = functools.reduce(jnp.maximum, pieces)
        total = sum(jnp.exp2((piece - peak) * scale) for piece in pieces)
        return peak + unit * jnp.log(total)

    ahead, behind = NZ // 2, NZ // 2 - 1

    piece_dims = dims // (CHUNKS * SHARERS)
    odd = lax.rem(mx, 2)
    sharers = [
        (my, mz, mc, mx + 1 - 2 * odd),
        (my, mz, mc, lax.rem(mx + NX - 1 + 2 * odd, NX)),
    ]

    def carried(source, h):
        first = pl.multiple_of((h * SHARERS + odd) * piece_dims, piece_dims)
        return gbuf.at[source, pl.ds(first, piece_dims)]

    def ring_copy(direction, source, s, h, device):
        piece = carried(source, h)
        return remote(piece, piece, ring_s.at[direction, s, h], ring_r.at[direction, s, h], device)

    def right(s, h):
        return ring_copy(0, from_z(s), s, h, at_z(1))

    def left(s, h):
        return ring_copy(1, lax.rem(mz + s, NZ), s, h, at_z(NZ - 1))

    def source_of(p):
        s = (p + 1) // 2
        return from_z(s) if p % 2 else lax.rem(mz + s, NZ)

    def share(p, h):
        piece = carried(source_of(p), h)
        return remote(piece, piece, share_s.at[h, p], share_r.at[h, p], sharers[h])

    unspread = list(range(NZ))

    def spread(p):
        if p in unspread:
            unspread.remove(p)
            if p:
                for h in range(CHUNKS):
                    share(p, h).wait_recv()
            xg_all[p, 0:dims, :] = gbuf[source_of(p)].astype(BF16)

    turns = [(s, h) for s in range(ahead + 1) for h in range(CHUNKS)]

    def turn(count=1):
        for _ in range(min(count, len(turns))):
            s, h = turns.pop(0)
            if 0 < s <= ahead:
                right(s - 1, h).wait_recv()
            if s < ahead:
                right(s, h).start()
            if 0 < s <= ahead:
                share(2 * s - 1, h).start()
            if 0 < s <= behind:
                left(s - 1, h).wait_recv()
            if s < behind:
                left(s, h).start()
            if 0 < s <= behind:
                share(2 * s, h).start()
            if h == CHUNKS - 1:
                for p in (2 * s - 5, 2 * s - 4):
                    if p >= 0:
                        spread(p)

    f_pass(fx.at[0, mx], 0, rows // tall)
    pl.semaphore_wait(barrier, NX + NZ + NY - 2)

    def f_copy(it, k):
        slot = fx.at[it, mx]
        return remote(slot, slot, f_s.at[it, k - 1], f_r.at[it, k - 1], at_x(k))

    def z_copy(k):
        slot = gz.at[mz]
        return remote(slot, slot, gz_s.at[k], gz_r.at[k], at_z(k))

    def a_copy(k):
        slot = av.at[mz]
        return remote(slot, slot, av_s.at[k], av_r.at[k], at_z(k))

    def g2_copy(k):
        slot = g2.at[mc, mz]
        return remote(slot, slot, g2_s.at[k], g2_r.at[k], at_z(k))

    gp_copy = remote(gpart.at[other], gpair, gp_s, gp_r, pair)
    gb_copy = remote(bfull.at[mc], bfull.at[mc], gb_s, gb_r, pair)

    def f_exchange(it):
        for k in range(1, NX):
            f_copy(it, k).start()
        turn(2)
        for k in range(1, NX):
            f_copy(it, k).wait_recv()
        return log_cells - merged([fx[it, k] for k in range(NX)])

    a = f_exchange(0)
    put_a(xt_g, a)
    count = columns // step
    for first in range(0, count, 2):
        g_pass(first, first + 2)
        if first + 4 == count:
            turn()
    gp_copy.start()
    turn()
    gp_copy.wait_recv()
    gz[mz] = merged([gpart[mc], gpair[...]])
    each(NZ - 1, lambda i: z_copy(far_first(i)).start())
    turn(GZ)
    each(NZ - 1, lambda i: z_copy(i + 1).wait_recv())
    bfull[mc] = log_support - merged([gz[k] for k in range(NZ)])
    gb_copy.start()
    gb_copy.wait_recv()
    for h in range(NC):
        for r in range(NZ):
            j = (h * NZ + r) * 128
            yf[dims : dims + GUARD, j : j + 128] = three_rows(bfull[h, r : r + 1], GUARD).astype(BF16)
    turn()
    f_pass(fx.at[1, mx], 0, 1)
    turn()
    f_pass(fx.at[1, mx], 1, rows // tall)
    a = f_exchange(1)
    av[mz] = a
    out_f[...] = (a + half_x) * (2.0 / dims)
    each(NZ - 1, lambda i: a_copy(far_first(i)).start())
    for h in range(NC):
        at = pl.ds(pl.multiple_of(h * half + mz * 128, 128), 128)
        y_own[h * 128 : (h + 1) * 128, :] = jnp.transpose(yc[:, at].astype(F32)).astype(BF16)
    turn(AV)
    each(NZ - 1, lambda i: a_copy(i + 1).wait_recv())

    def weigh(first, carry):
        top, total = carry
        weights = y_own[...]
        products, blocks = [], []
        for p in range(first, first + GROUP):
            rows16 = three_rows(av[source_of(p)], GUARD)
            i16 = lax.broadcasted_iota(jnp.int32, rows16.shape, 0)
            xg_all[p, dims : dims + GUARD, :] = jnp.where(i16 == 3, 1.0, rows16).astype(BF16)
            blocks.append(xg_all[p])
            products.append(jnp.dot(weights, blocks[-1], preferred_element_type=F32))
        tiles = [x[:, k : k + 128] for x in products for k in range(0, rows, 128)]
        peak = jnp.max(functools.reduce(jnp.maximum, tiles), axis=1, keepdims=True)
        peak = jnp.maximum(top, peak)
        total = total * jnp.exp2((top - peak) * scale)
        for logits, block in zip(products, blocks):
            plan = jnp.exp2((logits - peak) * scale)
            hi = plan.astype(BF16)
            low = (plan - hi.astype(F32)).astype(BF16)
            for half_plan in (hi, low):
                total = total + lax.dot_general(
                    half_plan, block, (((1,), (1,)), ((), ())), preferred_element_type=F32
                )
        return peak, total

    wide_j = NC * 128
    carry = jnp.full((wide_j, 1), LOW, F32), jnp.zeros((wide_j, DEPTH), F32)
    for first in range(0, NZ, GROUP):
        while turns and turns[0][0] <= (first + GROUP) // 2:
            turn()
        for p in range(first, first + GROUP):
            spread(p)
        carry = weigh(first, carry)
    top, total = carry
    row_mass, row_top, lines = dims + 3, dims + 4, dims + 8
    lane_u = lax.broadcasted_iota(jnp.int32, (wide_j, DEPTH), 1)
    total = jnp.where(lane_u == row_top, top, total)
    for h in range(NC):
        usend[h] = jnp.transpose(total[h * 128 : (h + 1) * 128])[0:lines]
    u_copy = remote(usend.at[other], urecv, u_s, u_r, pair)
    u_copy.start()
    u_copy.wait_recv()
    mine, theirs = usend[mc], urecv[...]
    top_one, top_two = mine[row_top : row_top + 1], theirs[row_top : row_top + 1]
    peak = jnp.maximum(top_one, top_two)
    total = mine * jnp.exp2((top_one - peak) * scale) + theirs * jnp.exp2((top_two - peak) * scale)
    mass = total[row_mass : row_mass + 1]
    tsend[...] = total[0:dims] / mass

    def t_copy(k):
        at = pl.ds(pl.multiple_of(lax.rem(my + k, NY) * part, part), part)
        return remote(tsend.at[at], ty.at[my], ty_s.at[k - 1], ty_r.at[k - 1], at_y(k))

    for k in range(1, NY):
        t_copy(k).start()
    g2[mc, mz] = log_support - peak - unit * jnp.log(mass)
    each(NZ - 1, lambda i: g2_copy(far_first(i)).start())
    band = pl.ds(pl.multiple_of(my * part, part), part)
    ty[my] = tsend[band, :]
    for k in range(1, NY):
        t_copy(k).wait_recv()

    def place(z):
        return out_n.at[band, pl.ds(pl.multiple_of(mc * half + z * 128, 128), 128)]

    place(mz)[...] = sum(ty[k] for k in range(NY)) * (1.0 / NY)

    def n_copy(k):
        return remote(place(mz), place(mz), nz_s.at[k], nz_r.at[k], at_z(k))

    each(NZ - 1, lambda i: n_copy(far_first(i)).start())

    def forward(z):
        for k in range(1, NY):
            remote(place(z), place(z), ny_s.at[k - 1], ny_r.at[k - 1], at_y(k)).start()

    forward(mz)

    for it in range(ITERS):
        for k in range(1, NX):
            f_copy(it, k).wait_send()
    for copy in (gp_copy, gb_copy, u_copy):
        copy.wait_send()
    for h in range(CHUNKS):
        for p in range(1, NZ):
            share(p, h).wait_send()
        for s in range(ahead):
            right(s, h).wait_send()
        for s in range(behind):
            left(s, h).wait_send()

    def left_early(i):
        for copy in (z_copy, a_copy):
            copy(i + 1).wait_send()

    each(NZ - 1, left_early)

    def arrived(i):
        k = far_first(NZ - 2 - i)
        n_copy(k).wait_recv()
        forward(from_z(k))

    each(NZ - 1, arrived)
    own_half = pl.ds(pl.multiple_of(mc * half, half), half)

    def strip(y):
        return out_n.at[pl.ds(pl.multiple_of(y * part, part), part), own_half]

    def np_copy(k):
        piece = strip(lax.rem(my + NY - k, NY))
        return remote(piece, piece, np_s.at[k], np_r.at[k], pair)

    np_copy(0).start()
    each(NZ - 1, lambda i: g2_copy(i + 1).wait_recv())
    g2p_copy = remote(g2.at[mc], g2.at[mc], g2p_s, g2p_r, pair)
    g2p_copy.start()

    def ny_whole(k):
        piece = strip(lax.rem(my + NY - k, NY))
        return remote(piece, piece, ny_s.at[k - 1], ny_r.at[k - 1], at_y(k))

    for k in range(1, NY):
        ny_whole(k).wait_recv()
        np_copy(k).start()
    g2p_copy.wait_recv()
    for h in range(NC):
        for r in range(NZ):
            at = slice((h * NZ + r) * 128, (h * NZ + r + 1) * 128)
            out_g[:, at] = (g2[h, r] + half_y[:, at]) * (2.0 / dims)
    for k in range(NY):
        np_copy(k).wait_recv()

    for k in range(1, NY):
        t_copy(k).wait_send()
        ny_whole(k).wait_send()
    for k in range(NY):
        np_copy(k).wait_send()
    g2p_copy.wait_send()

    def left_z(i):
        for copy in (g2_copy, n_copy):
            copy(i + 1).wait_send()

    each(NZ - 1, left_z)


def solution(mesh):
    NY, NX = mesh.shape["atlas"], mesh.shape["col"]
    NC = 2
    NZ = mesh.shape["row"] // NC
    split = Mesh(mesh.devices.reshape(NY, NZ, NC, NX), AXES)
    dma = pltpu.SemaphoreType.DMA

    def shards(cells, support):
        dims, rows = cells.shape[1:]
        columns = support.shape[1]
        part = dims // NY
        lines = dims + 8
        vmem = pltpu.VMEM
        scratch = [
            vmem((1, dims, rows), BF16),
            vmem((dims, columns), BF16),
            dma((2,)),
            vmem((rows, DEPTH), BF16),
            vmem((rows, DEPTH), BF16),
            vmem((DEPTH, columns), BF16),
            vmem((DEPTH, columns), BF16),
            vmem((1, columns), F32),
            vmem((NZ, dims, rows), F32),
            vmem((NZ, DEPTH, rows), BF16),
            vmem((NC * 128, DEPTH), BF16),
            vmem((ITERS, NX, 1, rows), F32),
            vmem((NC, NZ, 128), F32),
            vmem((NZ, 128), F32),
            vmem((NZ, NZ, 128), F32),
            vmem((NC, NZ, 128), F32),
            vmem((NZ, 1, rows), F32),
            vmem((NC, lines, 128), F32),
            vmem((lines, 128), F32),
            vmem((dims, 128), F32),
            vmem((NY, part, 128), F32),
            vmem((NC, NZ, 1, 128), F32),
            dma((ITERS, NX - 1)), dma((ITERS, NX - 1)),
            dma, dma,
            dma((NZ,)), dma((NZ,)),
            dma, dma,
            dma((NZ,)), dma((NZ,)),
            dma((2, NZ // 2, CHUNKS)), dma((2, NZ // 2, CHUNKS)),
            dma((CHUNKS, NZ)), dma((CHUNKS, NZ)),
            dma, dma,
            dma((NY - 1,)), dma((NY - 1,)),
            dma((NZ,)), dma((NZ,)),
            dma, dma,
            dma((NZ,)), dma((NZ,)),
            dma((NY - 1,)), dma((NY - 1,)),
            dma((NY,)), dma((NY,)),
        ]
        body = functools.partial(kernel, (NY, NZ, NC, NX), rows * NZ * NC, columns * NX)
        shapes = (
            jax.ShapeDtypeStruct((1, rows), F32),
            jax.ShapeDtypeStruct((1, columns), F32),
            jax.ShapeDtypeStruct((dims, columns), F32),
        )
        return pl.pallas_call(
            body,
            out_shape=[pltpu.VMEM(shape.shape, F32) for shape in shapes],
            in_specs=[pl.BlockSpec(memory_space=pl.ANY)] * 2,
            out_specs=[pl.BlockSpec(memory_space=pltpu.VMEM)] * 3,
            scratch_shapes=scratch,
            compiler_params=pltpu.CompilerParams(
                collective_id=0, has_side_effects=True, vmem_limit_bytes=56 << 20
            ),
        )(cells, support)

    row = ("row_0", "row_1")
    in_specs = (P("atlas", None, row), P(None, "col"))
    out_specs = (P("atlas", row), P("atlas", "col"), P(None, "col"))
    return jax.shard_map(shards, mesh=split, in_specs=in_specs, out_specs=out_specs, check_vma=False)
```

```python
import functools
import math

import jax
import jax.numpy as jnp
from jax import lax
from jax.experimental import pallas as pl
from jax.experimental.pallas import tpu as pltpu
from jax.sharding import Mesh
from jax.sharding import PartitionSpec as P

ITERS = 2
BLUR = 0.1
AXES = ("atlas", "row_0", "row_1", "col")
F32, BF16 = jnp.float32, jnp.bfloat16
LOW = -1e30
DEPTH = 128
GUARD = 16
GZ = 6
AV = 4
CHUNKS = 2
SHARERS = 2
GROUP = 4


def remote(src, dst, send, recv, device):
    return pltpu.make_async_remote_copy(
        src_ref=src,
        dst_ref=dst,
        send_sem=send,
        recv_sem=recv,
        device_id=device,
        device_id_type=pl.DeviceIdType.MESH,
    )


def three_rows(v, rows):
    hi = v.astype(BF16).astype(F32)
    rest = v - hi
    mid = rest.astype(BF16).astype(F32)
    low = rest - mid
    i = lax.broadcasted_iota(jnp.int32, (rows, v.shape[1]), 0)
    return jnp.where(i == 0, hi, jnp.where(i == 1, mid, jnp.where(i == 2, low, 0.0)))


def kernel(sizes, total_cells, total_support, *refs):
    (
        cells_in, support_in, out_f, out_g, out_n, cells, support, in_sem,
        xt_f, xt_g, yc, yf, half_y, gbuf, xg_all, y_own, plans,
        fx, gpart, gpair, gz, bfull, av, usend, urecv, tsend, ty, g2,
        f_s, f_r, gp_s, gp_r, gz_s, gz_r, gb_s, gb_r, av_s, av_r,
        ring_s, ring_r, share_s, share_r, u_s, u_r, ty_s, ty_r, g2_s, g2_r, g2p_s, g2p_r,
        nz_s, nz_r, ny_s, ny_r, np_s, np_r,
    ) = refs
    NY, NZ, NC, NX = sizes
    my, mz, mc, mx = (lax.axis_index(a) for a in AXES)
    dims, rows = cells_in.shape[1:]
    columns = support_in.shape[1]
    half = columns // NC
    part = dims // NY
    unit = dims * BLUR / 2.0
    scale = math.log2(math.e) / unit
    log_cells = unit * math.log(1.0 / total_cells)
    log_support = unit * math.log(1.0 / total_support)
    other = 1 - mc

    def at_z(k):
        return (my, lax.rem(mz + k, NZ), mc, mx)

    def at_y(k):
        return (lax.rem(my + k, NY), mz, mc, mx)

    def at_x(k):
        return (my, mz, mc, lax.rem(mx + k, NX))

    pair = (my, mz, other, mx)

    def from_z(k):
        return lax.rem(mz + NZ - k, NZ)

    def far_first(i):
        return NZ // 2 + (1 - 2 * lax.rem(i, 2)) * ((i + 1) // 2)

    def each(count, visit):
        def body(i, carry):
            visit(i)
            return carry

        lax.fori_loop(0, count, body, 0)

    barrier = pltpu.get_barrier_semaphore()

    def greet(device):
        pl.semaphore_signal(barrier, inc=1, device_id=device, device_id_type=pl.DeviceIdType.MESH)

    loads = [
        pltpu.make_async_copy(cells_in, cells, in_sem.at[0]),
        pltpu.make_async_copy(support_in, support, in_sem.at[1]),
    ]
    for load in loads:
        load.start()
    each(NZ - 1, lambda i: greet(at_z(far_first(i))))
    for k in range(1, NX):
        greet(at_x(k))
    for k in range(1, NY):
        greet(at_y(k))
    greet(pair)

    loads[0].wait()
    x32 = cells[0].astype(F32)
    gbuf[mz] = x32
    half_x = 0.5 * jnp.sum(x32 * x32, axis=0, keepdims=True)
    lane = lax.broadcasted_iota(jnp.int32, (128, DEPTH), 1)
    ones_lane = jnp.where((lane >= dims) & (lane < dims + 3), 1.0, 0.0)
    spare = jnp.zeros((DEPTH - dims, 128), F32)

    def turned(block):
        return jnp.transpose(jnp.concatenate([block, spare], axis=0))

    for r in range(0, rows, 128):
        t = turned(x32[:, r : r + 128])
        xt_g[r : r + 128, :] = t.astype(BF16)
        xt_f[r : r + 128, :] = (t + ones_lane).astype(BF16)
    step = 512
    for p in range(NZ):
        xg_all[p, dims + GUARD : DEPTH, :] = jnp.zeros((DEPTH - dims - GUARD, rows), BF16)

    def prepare(i):
        at = pl.ds(pl.multiple_of(i * step, step), step)
        y = support[:, at]
        yc[0:dims, at] = y
        yf[0:dims, at] = y
        i16 = lax.broadcasted_iota(jnp.int32, (GUARD, step), 0)
        yc[dims : dims + GUARD, at] = jnp.where(i16 < 3, 1.0, 0.0).astype(BF16)
        zeros = jnp.zeros((DEPTH - dims - GUARD, step), BF16)
        yc[dims + GUARD : DEPTH, at] = zeros
        yf[dims + GUARD : DEPTH, at] = zeros
        y32 = y.astype(F32)
        squares = 0.5 * jnp.sum(y32 * y32, axis=0, keepdims=True)
        half_y[:, at] = squares
        yf[dims : dims + GUARD, at] = three_rows(-squares, GUARD).astype(BF16)

    loads[1].wait()
    each(columns // step, prepare)

    def put_a(ref, a):
        ref[:, dims : dims + 8] = jnp.transpose(three_rows(a, 8)).astype(BF16)

    eye = lax.broadcasted_iota(jnp.int32, (128, 128), 0) == lax.broadcasted_iota(jnp.int32, (128, 128), 1)
    wide = 1024
    tall = min(256, rows)

    def f_pass(slot, first, last):
        def visit(r):
            r = r + first
            at = pl.ds(pl.multiple_of(r * tall, tall), tall)
            xt = xt_f[at, :]
            top = jnp.full((tall, 128), LOW, F32)
            total = jnp.zeros((tall, 128), F32)
            for c in range(0, columns, wide):
                logits = jnp.dot(xt, yf[:, c : c + wide], preferred_element_type=F32)
                tiles = [logits[:, k : k + 128] for k in range(0, wide, 128)]
                peak = functools.reduce(jnp.maximum, tiles, top)
                total = total * jnp.exp2((top - peak) * scale)
                for tile in tiles:
                    total = total + jnp.exp2((tile - peak) * scale)
                top = peak
            peak = jnp.max(top, axis=1, keepdims=True)
            total = jnp.sum(total * jnp.exp2((top - peak) * scale), axis=1, keepdims=True)
            lse = peak + unit * jnp.log(total)
            for k in range(tall // 128):
                piece = jnp.where(eye, lse[k * 128 : (k + 1) * 128], 0.0)
                row = jnp.sum(piece, axis=0, keepdims=True)
                slot[:, pl.ds(pl.multiple_of(r * tall + k * 128, 128), 128)] = row

        each(last - first, visit)

    def g_pass(first, last):
        high = min(256, rows)

        for i in range(first, last):
            w = yc[:, i * step : (i + 1) * step]
            top = jnp.full((8, step), LOW, F32)
            total = jnp.zeros((8, step), F32)
            for r in range(0, rows, high):
                logits = jnp.dot(xt_g[r : r + high, :], w, preferred_element_type=F32)
                logits = logits.reshape(high // 8, 8, step)
                peak = jnp.maximum(top, jnp.max(logits, axis=0))
                total = total * jnp.exp2((top - peak) * scale) + jnp.sum(
                    jnp.exp2((logits - peak[None]) * scale), axis=0
                )
                top = peak
            peak = jnp.max(top, axis=0, keepdims=True)
            total = jnp.sum(total * jnp.exp2((top - peak) * scale), axis=0, keepdims=True)
            lse = peak + unit * jnp.log(total)
            for k in range(step // 128):
                r = i * (step // 128) + k
                gpart[r // NZ, r % NZ : r % NZ + 1, :] = lse[:, k * 128 : (k + 1) * 128]

    def merged(pieces):
        peak = functools.reduce(jnp.maximum, pieces)
        total = sum(jnp.exp2((piece - peak) * scale) for piece in pieces)
        return peak + unit * jnp.log(total)

    ahead, behind = NZ // 2, NZ // 2 - 1

    piece_dims = dims // (CHUNKS * SHARERS)
    odd = lax.rem(mx, 2)
    sharers = [
        (my, mz, mc, mx + 1 - 2 * odd),
        (my, mz, mc, lax.rem(mx + NX - 1 + 2 * odd, NX)),
    ]

    def carried(source, h):
        first = pl.multiple_of((h * SHARERS + odd) * piece_dims, piece_dims)
        return gbuf.at[source, pl.ds(first, piece_dims)]

    def ring_copy(direction, source, s, h, device):
        piece = carried(source, h)
        return remote(piece, piece, ring_s.at[direction, s, h], ring_r.at[direction, s, h], device)

    def right(s, h):
        return ring_copy(0, from_z(s), s, h, at_z(1))

    def left(s, h):
        return ring_copy(1, lax.rem(mz + s, NZ), s, h, at_z(NZ - 1))

    def source_of(p):
        s = (p + 1) // 2
        return from_z(s) if p % 2 else lax.rem(mz + s, NZ)

    def share(p, h):
        piece = carried(source_of(p), h)
        return remote(piece, piece, share_s.at[h, p], share_r.at[h, p], sharers[h])

    unspread = list(range(NZ))

    def spread(p):
        if p in unspread:
            unspread.remove(p)
            if p:
                for h in range(CHUNKS):
                    share(p, h).wait_recv()
            xg_all[p, 0:dims, :] = gbuf[source_of(p)].astype(BF16)

    turns = [(s, h) for s in range(ahead + 1) for h in range(CHUNKS)]

    def turn(count=1):
        for _ in range(min(count, len(turns))):
            s, h = turns.pop(0)
            if 0 < s <= ahead:
                right(s - 1, h).wait_recv()
            if s < ahead:
                right(s, h).start()
            if 0 < s <= ahead:
                share(2 * s - 1, h).start()
            if 0 < s <= behind:
                left(s - 1, h).wait_recv()
            if s < behind:
                left(s, h).start()
            if 0 < s <= behind:
                share(2 * s, h).start()
            if h == CHUNKS - 1:
                for p in (2 * s - 5, 2 * s - 4):
                    if p >= 0:
                        spread(p)

    f_pass(fx.at[0, mx], 0, rows // tall)
    pl.semaphore_wait(barrier, NX + NZ + NY - 2)

    def f_copy(it, k):
        slot = fx.at[it, mx]
        return remote(slot, slot, f_s.at[it, k - 1], f_r.at[it, k - 1], at_x(k))

    def z_copy(k):
        slot = gz.at[mz]
        return remote(slot, slot, gz_s.at[k], gz_r.at[k], at_z(k))

    def a_copy(k):
        slot = av.at[mz]
        return remote(slot, slot, av_s.at[k], av_r.at[k], at_z(k))

    def g2_copy(k):
        slot = g2.at[mc, mz]
        return remote(slot, slot, g2_s.at[k], g2_r.at[k], at_z(k))

    gp_copy = remote(gpart.at[other], gpair, gp_s, gp_r, pair)
    gb_copy = remote(bfull.at[mc], bfull.at[mc], gb_s, gb_r, pair)

    def f_exchange(it):
        for k in range(1, NX):
            f_copy(it, k).start()
        turn(2)
        for k in range(1, NX):
            f_copy(it, k).wait_recv()
        return log_cells - merged([fx[it, k] for k in range(NX)])

    a = f_exchange(0)
    put_a(xt_g, a)
    count = columns // step
    for first in range(0, count, 2):
        g_pass(first, first + 2)
        if first + 4 == count:
            turn()
    gp_copy.start()
    turn()
    gp_copy.wait_recv()
    gz[mz] = merged([gpart[mc], gpair[...]])
    each(NZ - 1, lambda i: z_copy(far_first(i)).start())
    turn(GZ)
    each(NZ - 1, lambda i: z_copy(i + 1).wait_recv())
    bfull[mc] = log_support - merged([gz[k] for k in range(NZ)])
    gb_copy.start()
    gb_copy.wait_recv()
    for h in range(NC):
        for r in range(NZ):
            j = (h * NZ + r) * 128
            yf[dims : dims + GUARD, j : j + 128] = three_rows(bfull[h, r : r + 1], GUARD).astype(BF16)
    turn()
    f_pass(fx.at[1, mx], 0, 1)
    turn()
    f_pass(fx.at[1, mx], 1, rows // tall)
    a = f_exchange(1)
    av[mz] = a
    out_f[...] = (a + half_x) * (2.0 / dims)
    each(NZ - 1, lambda i: a_copy(far_first(i)).start())
    for h in range(NC):
        at = pl.ds(pl.multiple_of(h * half + mz * 128, 128), 128)
        y_own[h * 128 : (h + 1) * 128, :] = jnp.transpose(yc[:, at].astype(F32)).astype(BF16)
    turn(AV)
    each(NZ - 1, lambda i: a_copy(i + 1).wait_recv())

    def weigh(first, carry):
        top, total = carry
        weights = y_own[...]
        products, blocks = [], []
        for p in range(first, first + GROUP):
            rows16 = three_rows(av[source_of(p)], GUARD)
            i16 = lax.broadcasted_iota(jnp.int32, rows16.shape, 0)
            xg_all[p, dims : dims + GUARD, :] = jnp.where(i16 == 3, 1.0, rows16).astype(BF16)
            blocks.append(xg_all[p])
            products.append(jnp.dot(weights, blocks[-1], preferred_element_type=F32))
        tiles = [x[:, k : k + 128] for x in products for k in range(0, rows, 128)]
        peak = jnp.max(functools.reduce(jnp.maximum, tiles), axis=1, keepdims=True)
        peak = jnp.maximum(top, peak)
        total = total * jnp.exp2((top - peak) * scale)
        for logits, block in zip(products, blocks):
            plan = jnp.exp2((logits - peak) * scale)
            hi = plan.astype(BF16)
            low = (plan - hi.astype(F32)).astype(BF16)
            for half_plan in (hi, low):
                total = total + lax.dot_general(
                    half_plan, block, (((1,), (1,)), ((), ())), preferred_element_type=F32
                )
        return peak, total

    wide_j = NC * 128
    carry = jnp.full((wide_j, 1), LOW, F32), jnp.zeros((wide_j, DEPTH), F32)
    for first in range(0, NZ, GROUP):
        while turns and turns[0][0] <= (first + GROUP) // 2:
            turn()
        for p in range(first, first + GROUP):
            spread(p)
        carry = weigh(first, carry)
    top, total = carry
    row_mass, row_top, lines = dims + 3, dims + 4, dims + 8
    lane_u = lax.broadcasted_iota(jnp.int32, (wide_j, DEPTH), 1)
    total = jnp.where(lane_u == row_top, top, total)
    plans[...] = total
    usend[other] = jnp.transpose(plans[pl.ds(pl.multiple_of(other * 128, 128), 128), :])[0:lines]
    u_copy = remote(usend.at[other], urecv, u_s, u_r, pair)
    u_copy.start()
    usend[mc] = jnp.transpose(plans[pl.ds(pl.multiple_of(mc * 128, 128), 128), :])[0:lines]
    u_copy.wait_recv()
    mine, theirs = usend[mc], urecv[...]
    top_one, top_two = mine[row_top : row_top + 1], theirs[row_top : row_top + 1]
    peak = jnp.maximum(top_one, top_two)
    total = mine * jnp.exp2((top_one - peak) * scale) + theirs * jnp.exp2((top_two - peak) * scale)
    mass = total[row_mass : row_mass + 1]
    tsend[...] = total[0:dims] / mass

    def t_copy(k):
        at = pl.ds(pl.multiple_of(lax.rem(my + k, NY) * part, part), part)
        return remote(tsend.at[at], ty.at[my], ty_s.at[k - 1], ty_r.at[k - 1], at_y(k))

    for k in range(1, NY):
        t_copy(k).start()
    g2[mc, mz] = log_support - peak - unit * jnp.log(mass)
    each(NZ - 1, lambda i: g2_copy(far_first(i)).start())
    band = pl.ds(pl.multiple_of(my * part, part), part)
    ty[my] = tsend[band, :]
    for k in range(1, NY):
        t_copy(k).wait_recv()

    def place(z):
        return out_n.at[band, pl.ds(pl.multiple_of(mc * half + z * 128, 128), 128)]

    place(mz)[...] = sum(ty[k] for k in range(NY)) * (1.0 / NY)

    def n_copy(k):
        return remote(place(mz), place(mz), nz_s.at[k], nz_r.at[k], at_z(k))

    each(NZ - 1, lambda i: n_copy(far_first(i)).start())

    def forward(z):
        for k in range(1, NY):
            remote(place(z), place(z), ny_s.at[k - 1], ny_r.at[k - 1], at_y(k)).start()

    forward(mz)

    for it in range(ITERS):
        for k in range(1, NX):
            f_copy(it, k).wait_send()
    for copy in (gp_copy, gb_copy, u_copy):
        copy.wait_send()
    for h in range(CHUNKS):
        for p in range(1, NZ):
            share(p, h).wait_send()
        for s in range(ahead):
            right(s, h).wait_send()
        for s in range(behind):
            left(s, h).wait_send()

    def left_early(i):
        for copy in (z_copy, a_copy):
            copy(i + 1).wait_send()

    each(NZ - 1, left_early)

    def arrived(i):
        k = far_first(NZ - 2 - i)
        n_copy(k).wait_recv()
        forward(from_z(k))

    each(NZ - 1, arrived)
    own_half = pl.ds(pl.multiple_of(mc * half, half), half)

    def strip(y):
        return out_n.at[pl.ds(pl.multiple_of(y * part, part), part), own_half]

    def np_copy(k):
        piece = strip(lax.rem(my + NY - k, NY))
        return remote(piece, piece, np_s.at[k], np_r.at[k], pair)

    np_copy(0).start()
    each(NZ - 1, lambda i: g2_copy(i + 1).wait_recv())
    g2p_copy = remote(g2.at[mc], g2.at[mc], g2p_s, g2p_r, pair)
    g2p_copy.start()

    def ny_whole(k):
        piece = strip(lax.rem(my + NY - k, NY))
        return remote(piece, piece, ny_s.at[k - 1], ny_r.at[k - 1], at_y(k))

    for k in range(1, NY):
        ny_whole(k).wait_recv()
        np_copy(k).start()
    g2p_copy.wait_recv()
    for h in range(NC):
        for r in range(NZ):
            at = slice((h * NZ + r) * 128, (h * NZ + r + 1) * 128)
            out_g[:, at] = (g2[h, r] + half_y[:, at]) * (2.0 / dims)
    for k in range(NY):
        np_copy(k).wait_recv()

    for k in range(1, NY):
        t_copy(k).wait_send()
        ny_whole(k).wait_send()
    for k in range(NY):
        np_copy(k).wait_send()
    g2p_copy.wait_send()

    def left_z(i):
        for copy in (g2_copy, n_copy):
            copy(i + 1).wait_send()

    each(NZ - 1, left_z)


def handed_on(*refs):
    arrays, results, done = refs[:3], refs[3:6], refs[6]
    pieces = []
    for array, result in zip(arrays, results):
        lines = array.shape[0]
        for at in range(0, lines, 16):
            piece = slice(at, min(at + 16, lines))
            pieces.append((array.at[piece], result.at[piece]))
    copies = [pltpu.make_async_copy(*piece, done.at[k]) for k, piece in enumerate(pieces)]
    for copy in copies:
        copy.start()
    for copy in copies:
        copy.wait()


def solution(mesh):
    NY, NX = mesh.shape["atlas"], mesh.shape["col"]
    NC = 2
    NZ = mesh.shape["row"] // NC
    split = Mesh(mesh.devices.reshape(NY, NZ, NC, NX), AXES)
    dma = pltpu.SemaphoreType.DMA

    def shards(cells, support):
        dims, rows = cells.shape[1:]
        columns = support.shape[1]
        part = dims // NY
        lines = dims + 8
        vmem = pltpu.VMEM
        scratch = [
            vmem((1, dims, rows), BF16),
            vmem((dims, columns), BF16),
            dma((2,)),
            vmem((rows, DEPTH), BF16),
            vmem((rows, DEPTH), BF16),
            vmem((DEPTH, columns), BF16),
            vmem((DEPTH, columns), BF16),
            vmem((1, columns), F32),
            vmem((NZ, dims, rows), F32),
            vmem((NZ, DEPTH, rows), BF16),
            vmem((NC * 128, DEPTH), BF16),
            vmem((NC * 128, DEPTH), F32),
            vmem((ITERS, NX, 1, rows), F32),
            vmem((NC, NZ, 128), F32),
            vmem((NZ, 128), F32),
            vmem((NZ, NZ, 128), F32),
            vmem((NC, NZ, 128), F32),
            vmem((NZ, 1, rows), F32),
            vmem((NC, lines, 128), F32),
            vmem((lines, 128), F32),
            vmem((dims, 128), F32),
            vmem((NY, part, 128), F32),
            vmem((NC, NZ, 1, 128), F32),
            dma((ITERS, NX - 1)), dma((ITERS, NX - 1)),
            dma, dma,
            dma((NZ,)), dma((NZ,)),
            dma, dma,
            dma((NZ,)), dma((NZ,)),
            dma((2, NZ // 2, CHUNKS)), dma((2, NZ // 2, CHUNKS)),
            dma((CHUNKS, NZ)), dma((CHUNKS, NZ)),
            dma, dma,
            dma((NY - 1,)), dma((NY - 1,)),
            dma((NZ,)), dma((NZ,)),
            dma, dma,
            dma((NZ,)), dma((NZ,)),
            dma((NY - 1,)), dma((NY - 1,)),
            dma((NY,)), dma((NY,)),
        ]
        body = functools.partial(kernel, (NY, NZ, NC, NX), rows * NZ * NC, columns * NX)
        shapes = (
            jax.ShapeDtypeStruct((1, rows), F32),
            jax.ShapeDtypeStruct((1, columns), F32),
            jax.ShapeDtypeStruct((dims, columns), F32),
        )
        found = pl.pallas_call(
            body,
            out_shape=[pltpu.VMEM(shape.shape, F32) for shape in shapes],
            in_specs=[pl.BlockSpec(memory_space=pl.ANY)] * 2,
            out_specs=[pl.BlockSpec(memory_space=pltpu.VMEM)] * 3,
            scratch_shapes=scratch,
            compiler_params=pltpu.CompilerParams(
                collective_id=0, has_side_effects=True, vmem_limit_bytes=56 << 20
            ),
        )(cells, support)
        return pl.pallas_call(
            handed_on,
            out_shape=shapes,
            in_specs=[pl.BlockSpec(memory_space=pl.ANY)] * 3,
            out_specs=[pl.BlockSpec(memory_space=pl.ANY)] * 3,
            scratch_shapes=[dma((2 + dims // 16,))],
            compiler_params=pltpu.CompilerParams(vmem_limit_bytes=1 << 20),
        )(*found)

    row = ("row_0", "row_1")
    in_specs = (P("atlas", None, row), P(None, "col"))
    out_specs = (P("atlas", row), P("atlas", "col"), P(None, "col"))
    return jax.shard_map(shards, mesh=split, in_specs=in_specs, out_specs=out_specs, check_vma=False)
```
